512 devices in a mesh: dp: 32 (over x, z_lo, core), shard: 16 (over y, z_hi).
Axes of the slice: x: 4, y: 8, z: 8 (z_hi: 2, z_lo: 4; z = z_hi * 4 + z_lo), core: 2. Of those that a mesh axis runs over, the one named last changes fastest.
Arguments:
- tokens: bfloat16 [98304, 4096], P(('dp', 'shard')), may hold values from -24 to 24
- cotangent: bfloat16 [98304, 512], P(('dp', 'shard')), may hold values from -6 to 6
- weight: bfloat16 [4096, 512], P('shard'), may hold values from -0.09375 to 0.09375
- moment_codes: bfloat16 [4096, 512], P('shard'), may hold values from -1 to 1
- moment_scale: float32 [1024], P('shard'), may hold values from 1 to 10
- second_codes: bfloat16 [4096, 512], P('shard'), may hold values from 0.25 to 1
- second_scale: float32 [1024], P('shard'), may hold values from 1 to 10
Outputs:
- input_grad: bfloat16 [98304, 4096], P(('dp', 'shard'))
- values_new: bfloat16 [98304, 512], P(('dp', 'shard'))
- moment_codes_new: bfloat16 [4096, 512], P('shard')
- second_codes_new: bfloat16 [4096, 512], P('shard')
The draws below stay inside these ranges and needn't reach their ends.
All inputs are finite; a program needn't handle non-finite values. Where the reference program divides by a largest or mean magnitude, that divisor is 1e-20 or more.
Results may differ from the reference program's by a relative error of at most 0.024.
Values may be sent and summed in bfloat16 or wider, within the bound.
No kernel may reach another device: no remote copies, remote signals or barrier semaphores. Data moves between devices by JAX's collectives and lax.ppermute only.
A program may use at most 64 MiB of HBM per device.

```python
import math
import jax
import jax.numpy as jnp
from jax import lax

DW = 4096
KV = 512
BLOCK = 2048
TOK_DEV = 192
TOKENS = 98304
BLOCKS = 1024
N_DP = 32


def with_spikes(array, key, source, target, blocks, factor):
    owner, partner = [(jnp.arange(array.shape[axis_at]) // (array.shape[axis_at] // blocks)).reshape([-1 if axis == axis_at else 1 for axis in range(array.ndim)]) for axis_at in (source, target)]
    chosen = jax.random.permutation(key, blocks)[partner]
    strong = (owner == chosen) | (owner == (partner + blocks // 2) % blocks)
    return jnp.where(strong, factor * array, array)


def levels(stream_key, dims, cuts, low, top_value):
    factor_of, own = 1.0, jax.random.fold_in(stream_key, 6)
    for axis_at, shards_of in cuts:
        heights = jnp.exp(jax.random.uniform(jax.random.fold_in(own, axis_at), (shards_of,), jnp.float32, low / len(cuts), top_value / len(cuts)))
        factor_of = factor_of * jnp.repeat(heights, dims[axis_at] // shards_of).reshape([-1 if axis == axis_at else 1 for axis in range(len(dims))])
    return factor_of


def scatter_about(own_key, dims, spread, most, split=(), kind=jnp.bfloat16):
    factor_of = levels(own_key, dims, split, -0.22, 0.18) if split else 1.0
    values = jax.random.normal(own_key, dims, jnp.float32) * spread * factor_of
    return jnp.minimum(jnp.maximum(values, -most), most).astype(kind)


def bell_draw_with(rng, shape, spread, reach, pieces, heavy, dtype=jnp.bfloat16):
    drawn = spread * jax.random.normal(rng, shape, jnp.float32)
    if pieces:
        drawn = drawn * levels(rng, shape, pieces, -0.22, 0.18)
    return jnp.clip(with_spikes(drawn, jax.random.fold_in(rng, 3), *heavy), -reach, reach).astype(dtype)


def setup_inputs(seed: int = 0) -> dict:
    keys = jax.random.split(jax.random.key(seed), 8)
    tokens = bell_draw_with(keys[0], (TOKENS, DW), 1.0, 24.0, ((0, 512),), (0, 1, 512, 6.0))
    cotangent = scatter_about(keys[1], (TOKENS, KV), 1.0, 6.0, ((0, 512),))
    weight = scatter_about(keys[2], (DW, KV), DW ** -0.5, 0.09375, ((0, 16),))
    moment_codes = jnp.clip(jax.random.uniform(keys[3], (DW, KV), jnp.float32, -1.0, 1.0) * levels(keys[3], (DW, KV), ((0, 16),), -0.4, 0.0), -1.0, 1.0).astype(jnp.bfloat16)
    moment_scale = jnp.clip(jnp.exp(math.log(10.0) - 2.3025851 * jax.random.uniform(keys[4], (BLOCKS,), jnp.float32) ** levels(keys[4], (BLOCKS,), ((0, 16),), -0.2, 0.2)), 1.0, 10.0)
    second_codes = jnp.clip(0.25 + 0.75 * jax.random.uniform(keys[5], (DW, KV), jnp.float32) ** levels(keys[5], (DW, KV), ((0, 16),), -0.2, 0.2), 0.25, 1.0).astype(jnp.bfloat16)
    second_scale = jnp.clip(jnp.exp(math.log(10.0) - 2.3025851 * jax.random.uniform(keys[6], (BLOCKS,), jnp.float32) ** levels(keys[6], (BLOCKS,), ((0, 16),), -0.2, 0.2)), 1.0, 10.0)
    return {"tokens": tokens, "cotangent": cotangent, "weight": weight, "moment_codes": moment_codes, "moment_scale": moment_scale, "second_codes": second_codes, "second_scale": second_scale}


beta_one = 0.9
beta_two = 0.95
learn_rate = 0.004
adam_eps = 1e-08
scale_eps = 1e-06

def reference(tokens, cotangent, weight, moment_codes, moment_scale, second_codes, second_scale):
    input_grad = jnp.dot(cotangent, weight.T, preferred_element_type=jnp.float32).astype(jnp.bfloat16)
    block_count = TOKENS // TOK_DEV
    token_blocks = tokens.reshape(block_count, TOK_DEV, DW)
    grad_blocks = cotangent.reshape(block_count, TOK_DEV, KV)

    def add_block(total, pair):
        term = jnp.dot(pair[0].T, pair[1], preferred_element_type=jnp.float32).astype(jnp.bfloat16)
        return (total + lax.optimization_barrier(term).astype(jnp.float32), None)
    summed, unused = lax.scan(add_block, jnp.zeros((DW, KV), jnp.float32), (token_blocks, grad_blocks))
    grad = (summed / N_DP).reshape(BLOCKS, BLOCK)
    moment = moment_codes.astype(jnp.float32).reshape(BLOCKS, BLOCK) * moment_scale[:, None]
    second = second_codes.astype(jnp.float32).reshape(BLOCKS, BLOCK) * second_scale[:, None]
    moment_new = beta_one * moment + (1.0 - beta_one) * grad
    second_new = beta_two * second + (1.0 - beta_two) * grad * grad
    old = weight.astype(jnp.float32).reshape(BLOCKS, BLOCK)
    weight_new = (old - learn_rate * moment_new / (jnp.sqrt(second_new) + adam_eps)).reshape(DW, KV).astype(jnp.bfloat16)
    moment_top = lax.optimization_barrier(jnp.max(jnp.abs(moment_new), axis=1)) + scale_eps
    second_top = lax.optimization_barrier(jnp.max(jnp.abs(second_new), axis=1)) + scale_eps
    moment_codes_new = (moment_new / moment_top[:, None]).reshape(DW, KV).astype(jnp.bfloat16)
    second_codes_new = (second_new / second_top[:, None]).reshape(DW, KV).astype(jnp.bfloat16)
    values_new = jnp.dot(tokens, weight_new, preferred_element_type=jnp.float32).astype(jnp.bfloat16)
    return (input_grad, values_new, moment_codes_new, second_codes_new)
```

```python
import jax
import jax.numpy as jnp
from jax import lax
from jax.sharding import Mesh
from jax.sharding import PartitionSpec as P

beta_one = 0.9
beta_two = 0.95
learn_rate = 0.004
adam_eps = 1e-08
scale_eps = 1e-06

X, ZL, C, Y, ZH = 4, 4, 2, 8, 2
AXES = ("x", "zl", "c", "y", "zh")
DP = X * ZL * C
F32, BF16 = jnp.float32, jnp.bfloat16

TURN = [
    ((x * C + c) * Y + y, ((y // C) * C + y % C) * Y + (x * C + c))
    for x in range(X)
    for c in range(C)
    for y in range(Y)
]
SWAP = [(0, 1), (1, 0)]


def a2a(a, axes):
    return lax.all_to_all(a, axes, 0, 0, tiled=True)


def to_all(a, axes, n):
    return a2a(jnp.broadcast_to(a[None], (n,) + a.shape), axes)


def local(tokens, cotangent, weight, moment_codes, moment_scale, second_codes, second_scale):
    x, c = lax.axis_index("x"), lax.axis_index("c")
    rows, kv = weight.shape
    tok, dw = tokens.shape
    chip = dw // X
    half = chip // C
    piece = half // (Y * ZH)
    per = 2048 // kv

    old_half = lax.dynamic_slice_in_dim(weight, c * (kv // 2), kv // 2, 1)
    old_half = lax.all_gather(old_half, ("y", "zh"), axis=0, tiled=True)

    turn_at = (x * C + c) * piece
    moment = moment_codes.astype(F32).reshape(-1, per, kv) * moment_scale[:, None, None]
    second = second_codes.astype(F32).reshape(-1, per, kv) * second_scale[:, None, None]
    state = jnp.stack([moment.reshape(rows, kv), second.reshape(rows, kv), weight.astype(F32)])
    state = lax.dynamic_slice_in_dim(state, turn_at, piece, 1)
    state = lax.ppermute(state, ("x", "c", "y"), TURN)

    send = jnp.concatenate(
        [
            tokens.reshape(tok, X, chip).transpose(1, 0, 2),
            jnp.broadcast_to(cotangent[None], (X, tok, kv)),
        ],
        axis=2,
    )
    got = a2a(send, "x").reshape(X * tok, chip + kv)
    cot = got[:, chip:]
    mine = lax.dynamic_slice_in_dim(got, c * half, half, 1)
    other = lax.dynamic_slice_in_dim(got, (1 - c) * half, half, 1)
    contract = (((0,), (0,)), ((), ()))
    away = lax.dot_general(other, cot, contract, preferred_element_type=F32).astype(BF16)
    away = lax.ppermute(away, "c", SWAP)
    grad = lax.dot_general(mine, cot, contract, preferred_element_type=F32) + away.astype(F32)
    grad = grad.astype(BF16).reshape(ZH, Y, piece, kv).transpose(1, 0, 2, 3)
    grad = jnp.sum(a2a(grad, "y").astype(F32), axis=0).astype(BF16)
    grad = jnp.broadcast_to(grad[None], (ZL, ZH, piece, kv)).reshape(ZL * ZH, piece, kv)
    grad = jnp.sum(a2a(grad, ("zl", "zh")).astype(F32), axis=0) / DP

    grad = grad.reshape(-1, per, kv)
    moment, second, old = (state[i].reshape(-1, per, kv) for i in range(3))
    moment_new = beta_one * moment + (1.0 - beta_one) * grad
    second_new = beta_two * second + (1.0 - beta_two) * grad * grad
    new = (old - learn_rate * moment_new / (jnp.sqrt(second_new) + adam_eps)).astype(BF16)
    moment_top = jnp.max(jnp.abs(moment_new), axis=(1, 2), keepdims=True) + scale_eps
    second_top = jnp.max(jnp.abs(second_new), axis=(1, 2), keepdims=True) + scale_eps
    codes = jnp.stack([moment_new / moment_top, second_new / second_top]).astype(BF16)

    new = to_all(new.reshape(piece, kv), ("zh", "y"), ZH * Y).reshape(half, kv)
    new_other = lax.ppermute(new, "c", SWAP)
    part = jnp.dot(mine, new, preferred_element_type=F32)
    part = part + jnp.dot(other, new_other, preferred_element_type=F32)
    part = a2a(part.astype(BF16).reshape(X, tok, kv), "x")
    values = jnp.sum(part.astype(F32), axis=0).astype(BF16)

    codes = lax.ppermute(codes.reshape(2, piece, kv), ("x", "c", "y"), TURN)
    codes = to_all(codes, ("x", "c"), X * C).reshape(X * C, 2, piece, kv)
    moment_out = codes[:, 0].reshape(rows, kv)
    second_out = codes[:, 1].reshape(rows, kv)

    old_other = lax.ppermute(old_half, "c", SWAP)
    old_all = jnp.where(
        c == 0,
        jnp.concatenate([old_half, old_other], axis=1),
        jnp.concatenate([old_other, old_half], axis=1),
    )
    input_grad = lax.dot_general(
        cotangent, old_all, (((1,), (1,)), ((), ())), preferred_element_type=F32
    ).astype(BF16)
    return (input_grad, values, moment_out, second_out)


def solution(mesh):
    fine = Mesh(mesh.devices.reshape(X, ZL, C, Y, ZH), AXES)
    tokens, state = P(AXES, None), P(("y", "zh"), None)
    scale = P(("y", "zh"))
    return jax.shard_map(
        local,
        mesh=fine,
        in_specs=(tokens, tokens, state, state, scale, state, scale),
        out_specs=(tokens, tokens, state, state),
        check_vma=False,
    )
```

```python
import jax
import jax.numpy as jnp
from jax import lax
from jax.sharding import Mesh
from jax.sharding import PartitionSpec as P

beta_one = 0.9
beta_two = 0.95
learn_rate = 0.004
adam_eps = 1e-08
scale_eps = 1e-06

X, ZL, C, Y, ZH = 4, 4, 2, 8, 2
AXES = ("x", "zl", "c", "y", "zh")
DP = X * ZL * C
F32, BF16 = jnp.float32, jnp.bfloat16

TURN, TURN_OTHER = (
    [
        ((x * C + c) * Y + y, ((y // C) * C + (y + flip) % C) * Y + (x * C + c))
        for x in range(X)
        for c in range(C)
        for y in range(Y)
    ]
    for flip in range(C)
)
SWAP = [(0, 1), (1, 0)]


def a2a(a, axes):
    return lax.all_to_all(a, axes, 0, 0, tiled=True)


def to_all(a, axes, n):
    return a2a(jnp.broadcast_to(a[None], (n,) + a.shape), axes)


def in_order(index, mine, other, axis):
    return jnp.where(
        index == 0,
        jnp.concatenate([mine, other], axis=axis),
        jnp.concatenate([other, mine], axis=axis),
    )


def local(tokens, cotangent, weight, moment_codes, moment_scale, second_codes, second_scale):
    x, c, zh = (lax.axis_index(name) for name in ("x", "c", "zh"))
    rows, kv = weight.shape
    tok, dw = tokens.shape
    chip = dw // X
    half = chip // C
    piece = half // (Y * ZH)
    per = 2048 // kv
    blocks = piece // per

    old_half = lax.dynamic_slice_in_dim(weight, c * (kv // 2), kv // 2, 1)
    old_half = in_order(zh, old_half, lax.ppermute(old_half, "zh", SWAP), 0)

    turn = x * C + c

    def decoded(code, scale):
        code = lax.dynamic_slice_in_dim(code, turn * piece, piece, 0)
        scale = lax.dynamic_slice_in_dim(scale, turn * blocks, blocks, 0)
        return code.astype(F32).reshape(blocks, per, kv) * scale[:, None, None]

    old = lax.dynamic_slice_in_dim(weight, turn * piece, piece, 0).astype(F32)
    state = jnp.stack(
        [
            decoded(moment_codes, moment_scale),
            decoded(second_codes, second_scale),
            old.reshape(blocks, per, kv),
        ]
    )
    state = lax.ppermute(state, ("x", "c", "y"), TURN)

    send = jnp.stack(
        [
            jnp.concatenate([tokens[:, i * chip : (i + 1) * chip], cotangent], axis=1)
            for i in range(X)
        ]
    )
    got = a2a(send, "x").reshape(X * tok, chip + kv)
    got, state, old_half = lax.optimization_barrier((got, state, old_half))
    old_half = lax.all_gather(old_half, "y", axis=0, tiled=True)
    cot = got[:, chip:]
    mine = lax.dynamic_slice_in_dim(got, c * half, half, 1)
    other = lax.dynamic_slice_in_dim(got, (1 - c) * half, half, 1)
    contract = (((0,), (0,)), ((), ()))
    away = lax.dot_general(other, cot, contract, preferred_element_type=F32).astype(BF16)
    away = lax.ppermute(away, "c", SWAP)
    grad = lax.dot_general(mine, cot, contract, preferred_element_type=F32) + away.astype(F32)
    grad = grad.astype(BF16).reshape(ZH, Y, piece, kv).transpose(1, 0, 2, 3)
    grad = jnp.sum(a2a(grad, "y").astype(F32), axis=0).astype(BF16)
    grad = jnp.broadcast_to(grad[None], (ZL, ZH, piece, kv)).reshape(ZL * ZH, piece, kv)
    grad = jnp.sum(a2a(grad, ("zl", "zh")).astype(F32), axis=0) / DP

    grad = grad.reshape(blocks, per, kv)
    moment, second, old = state[0], state[1], state[2]
    moment_new = beta_one * moment + (1.0 - beta_one) * grad
    second_new = beta_two * second + (1.0 - beta_two) * grad * grad
    new = (old - learn_rate * moment_new / (jnp.sqrt(second_new) + adam_eps)).astype(BF16)
    moment_top = jnp.max(jnp.abs(moment_new), axis=(1, 2), keepdims=True) + scale_eps
    second_top = jnp.max(jnp.abs(second_new), axis=(1, 2), keepdims=True) + scale_eps
    codes = jnp.stack([moment_new / moment_top, second_new / second_top]).astype(BF16)
    codes = codes.reshape(2 * piece, kv)

    new = to_all(new.reshape(piece, kv), ("zh", "y"), ZH * Y).reshape(half, kv)
    codes_same = lax.ppermute(codes, ("x", "c", "y"), TURN)
    codes_other = lax.ppermute(codes, ("x", "c", "y"), TURN_OTHER)
    new, codes_same, codes_other = lax.optimization_barrier((new, codes_same, codes_other))
    new_other = lax.ppermute(new, "c", SWAP)
    part = jnp.dot(mine, new, preferred_element_type=F32)
    part = part + jnp.dot(other, new_other, preferred_element_type=F32)
    part = part.astype(BF16).reshape(X, tok, kv)
    codes = in_order(c, codes_same, codes_other, 0)
    codes = jnp.broadcast_to(codes[None], (X,) + codes.shape)
    part = a2a(jnp.concatenate([part, codes], axis=1), "x")

    old_all = in_order(c, old_half, lax.ppermute(old_half, "c", SWAP), 1)
    input_grad = lax.dot_general(
        cotangent, old_all, (((1,), (1,)), ((), ())), preferred_element_type=F32
    ).astype(BF16)

    part, input_grad = lax.optimization_barrier((part, input_grad))
    values = jnp.sum(part[:, :tok].astype(F32), axis=0).astype(BF16)
    codes = part[:, tok:].reshape(X * C, 2, piece, kv)
    moment_out = codes[:, 0].reshape(rows, kv)
    second_out = codes[:, 1].reshape(rows, kv)
    return (input_grad, values, moment_out, second_out)


def solution(mesh):
    fine = Mesh(mesh.devices.reshape(X, ZL, C, Y, ZH), AXES)
    tokens, state = P(AXES, None), P(("y", "zh"), None)
    scale = P(("y", "zh"))
    return jax.shard_map(
        local,
        mesh=fine,
        in_specs=(tokens, tokens, state, state, scale, state, scale),
        out_specs=(tokens, tokens, state, state),
        check_vma=False,
    )
```

```python
import jax
import jax.numpy as jnp
from jax import lax
from jax.experimental import pallas as pl
from jax.sharding import Mesh
from jax.sharding import PartitionSpec as P

beta_one = 0.9
beta_two = 0.95
learn_rate = 0.004
adam_eps = 1e-08
scale_eps = 1e-06

X, ZL, C, Y, ZH = 4, 4, 2, 8, 2
AXES = ("x", "zl", "c", "y", "zh")
DP = X * ZL * C
F32, BF16 = jnp.float32, jnp.bfloat16

SWAP = [(0, 1), (1, 0)]
CROSS = [
    ((a * C + h) * ZH + h, ((ZL - 1 - a) * C + h) * ZH + 1 - h) for h in range(ZH) for a in range(ZL)
]


def a2a(a, axes):
    return lax.all_to_all(a, axes, 0, 0, tiled=True)


def to_all(a, axes, n):
    return a2a(jnp.broadcast_to(a[None], (n,) + a.shape), axes)


def in_order(index, mine, other, axis):
    return jnp.where(
        index == 0,
        jnp.concatenate([mine, other], axis=axis),
        jnp.concatenate([other, mine], axis=axis),
    )


def pack_kernel(tok_ref, cot_ref, out_ref):
    shard = tok_ref.shape[1] // (Y * ZH)
    run = shard // X
    for to in range(X):
        for h in range(ZH):
            for y in range(0, Y, 2):
                both = [
                    tok_ref[:, pl.ds((y + i) * ZH * shard + h * shard + to * run, run)]
                    for i in range(2)
                ]
                out_ref[to, :, pl.ds((h * Y + y) * run, 2 * run)] = jnp.concatenate(both, axis=1)
        out_ref[to, :, pl.ds(ZH * Y * run, cot_ref.shape[1])] = cot_ref[...]


def pack(tokens, cotangent):
    tok, dw = tokens.shape
    kv = cotangent.shape[1]
    block = tok // 4
    wide = dw // X + kv
    return pl.pallas_call(
        pack_kernel,
        grid=(tok // block,),
        in_specs=[
            pl.BlockSpec((block, dw), lambda i: (i, 0)),
            pl.BlockSpec((block, kv), lambda i: (i, 0)),
        ],
        out_specs=pl.BlockSpec((X, block, wide), lambda i: (0, i, 0)),
        out_shape=jax.ShapeDtypeStruct((X, tok, wide), BF16),
        cost_estimate=pl.CostEstimate(
            flops=0, bytes_accessed=2 * tok * (dw + kv + X * wide), transcendentals=0
        ),
    )(tokens, cotangent)


def local(tokens, cotangent, weight, moment_codes, moment_scale, second_codes, second_scale):
    x, c, zh = (lax.axis_index(name) for name in ("x", "c", "zh"))
    rows, kv = weight.shape
    tok, dw = tokens.shape
    chip = dw // X
    half = chip // C
    piece = half // Y
    per = 2048 // kv
    blocks = piece // per

    old_half = lax.dynamic_slice_in_dim(weight, c * (kv // 2), kv // 2, 1)
    old_half = in_order(zh, old_half, lax.ppermute(old_half, "zh", SWAP), 0)

    def decoded(code, scale):
        code = lax.dynamic_slice_in_dim(code, x * piece, piece, 0)
        scale = lax.dynamic_slice_in_dim(scale, x * blocks, blocks, 0)
        return code.astype(F32).reshape(blocks, per, kv) * scale[:, None, None]

    old = lax.dynamic_slice_in_dim(weight, x * piece, piece, 0).astype(F32)
    state = jnp.stack(
        [
            decoded(moment_codes, moment_scale),
            decoded(second_codes, second_scale),
            old.reshape(blocks, per, kv),
        ]
    )
    state = jnp.where(c == zh, state, lax.ppermute(state, ("zl", "c", "zh"), CROSS))

    got = a2a(pack(tokens, cotangent), "x").reshape(X * tok, chip + kv)
    got, state, old_half = lax.optimization_barrier((got, state, old_half))
    old_half = lax.all_gather(old_half, "y", axis=0, tiled=True)
    cot = got[:, chip:]
    mine = lax.dynamic_slice_in_dim(got, c * half, half, 1)
    other = lax.dynamic_slice_in_dim(got, (1 - c) * half, half, 1)
    contract = (((0,), (0,)), ((), ()))
    away = lax.dot_general(other, cot, contract, preferred_element_type=F32).astype(BF16)
    away = lax.ppermute(away, "c", SWAP)
    grad = lax.dot_general(mine, cot, contract, preferred_element_type=F32) + away.astype(F32)
    grad = a2a(grad.astype(BF16).reshape(Y, piece, kv), "y")
    grad = jnp.sum(grad.astype(F32), axis=0).astype(BF16)
    grad = jnp.sum(to_all(grad, ("zl", "zh"), ZL * ZH).astype(F32), axis=0) / DP

    grad = grad.reshape(blocks, per, kv)
    moment, second, old = state[0], state[1], state[2]
    moment_new = beta_one * moment + (1.0 - beta_one) * grad
    second_new = beta_two * second + (1.0 - beta_two) * grad * grad
    new = (old - learn_rate * moment_new / (jnp.sqrt(second_new) + adam_eps)).astype(BF16)
    moment_top = jnp.max(jnp.abs(moment_new), axis=(1, 2), keepdims=True) + scale_eps
    second_top = jnp.max(jnp.abs(second_new), axis=(1, 2), keepdims=True) + scale_eps
    codes = jnp.stack([moment_new / moment_top, second_new / second_top]).astype(BF16)
    codes = codes.reshape(2 * piece, kv)

    new = to_all(new.reshape(piece, kv), "y", Y).reshape(half, kv)
    codes = jnp.where(c == zh, codes, lax.ppermute(codes, "c", SWAP))
    new, codes, old_half = lax.optimization_barrier((new, codes, old_half))
    new_other = lax.ppermute(new, "c", SWAP)
    part = jnp.dot(mine, new, preferred_element_type=F32)
    part = part + jnp.dot(other, new_other, preferred_element_type=F32)
    part = part.astype(BF16).reshape(X, tok, kv)
    codes = jnp.broadcast_to(codes[None], (X,) + codes.shape)
    part = a2a(jnp.concatenate([part, codes], axis=1), "x")

    old_all = in_order(c, old_half, lax.ppermute(old_half, "c", SWAP), 1)
    input_grad = lax.dot_general(
        cotangent, old_all, (((1,), (1,)), ((), ())), preferred_element_type=F32
    ).astype(BF16)

    part, input_grad = lax.optimization_barrier((part, input_grad))
    values = jnp.sum(part[:, :tok].astype(F32), axis=0).astype(BF16)
    codes = part[:, tok:].reshape(X, 2, piece, kv)
    moment_out = codes[:, 0].reshape(rows, kv)
    second_out = codes[:, 1].reshape(rows, kv)
    return (input_grad, values, moment_out, second_out)


def solution(mesh):
    fine = Mesh(mesh.devices.reshape(X, ZL, C, Y, ZH), AXES)
    tokens, state = P(AXES, None), P(("y", "zh"), None)
    scale = P(("y", "zh"))
    return jax.shard_map(
        local,
        mesh=fine,
        in_specs=(tokens, tokens, state, state, scale, state, scale),
        out_specs=(tokens, tokens, state, state),
        check_vma=False,
    )
```

```python
import jax
import jax.numpy as jnp
from jax import lax
from jax.experimental import pallas as pl
from jax.sharding import Mesh
from jax.sharding import PartitionSpec as P

beta_one = 0.9
beta_two = 0.95
learn_rate = 0.004
adam_eps = 1e-08
scale_eps = 1e-06

X, ZL, C, Y, ZH = 4, 4, 2, 8, 2
AXES = ("x", "zl", "c", "y", "zh")
DP = X * ZL * C
F32, BF16 = jnp.float32, jnp.bfloat16

SWAP = [(0, 1), (1, 0)]
CROSS = [
    ((a * C + h) * ZH + h, ((ZL - 1 - a) * C + h) * ZH + 1 - h) for h in range(ZH) for a in range(ZL)
]


def a2a(a, axes):
    return lax.all_to_all(a, axes, 0, 0, tiled=True)


def to_all(a, axes, n):
    return a2a(jnp.broadcast_to(a[None], (n,) + a.shape), axes)


def in_order(index, mine, other, axis):
    return jnp.where(
        index == 0,
        jnp.concatenate([mine, other], axis=axis),
        jnp.concatenate([other, mine], axis=axis),
    )


def pack_kernel(tok_ref, cot_ref, out_ref):
    shard = tok_ref.shape[1] // (Y * ZH)
    run = shard // X
    for to in range(X):
        for h in range(ZH):
            for y in range(0, Y, 2):
                both = [
                    tok_ref[:, pl.ds((y + i) * ZH * shard + h * shard + to * run, run)]
                    for i in range(2)
                ]
                out_ref[to, :, pl.ds((h * Y + y) * run, 2 * run)] = jnp.concatenate(both, axis=1)
        out_ref[to, :, pl.ds(ZH * Y * run, cot_ref.shape[1])] = cot_ref[...]


def pack(tokens, cotangent):
    tok, dw = tokens.shape
    kv = cotangent.shape[1]
    block = tok // 2
    wide = dw // X + kv
    return pl.pallas_call(
        pack_kernel,
        grid=(tok // block,),
        in_specs=[
            pl.BlockSpec((block, dw), lambda i: (i, 0)),
            pl.BlockSpec((block, kv), lambda i: (i, 0)),
        ],
        out_specs=pl.BlockSpec((X, block, wide), lambda i: (0, i, 0)),
        out_shape=jax.ShapeDtypeStruct((X, tok, wide), BF16),
        cost_estimate=pl.CostEstimate(
            flops=0, bytes_accessed=2 * tok * (dw + kv + X * wide), transcendentals=0
        ),
    )(tokens, cotangent)


def local(tokens, cotangent, weight, moment_codes, moment_scale, second_codes, second_scale):
    x, c, zh = (lax.axis_index(name) for name in ("x", "c", "zh"))
    rows, kv = weight.shape
    tok, dw = tokens.shape
    chip = dw // X
    half = chip // C
    piece = half // Y
    per = 2048 // kv
    blocks = piece // per

    old_half = lax.dynamic_slice_in_dim(weight, c * (kv // 2), kv // 2, 1)
    old_half = in_order(zh, old_half, lax.ppermute(old_half, "zh", SWAP), 0)

    def decoded(code, scale):
        code = lax.dynamic_slice_in_dim(code, x * piece, piece, 0)
        scale = lax.dynamic_slice_in_dim(scale, x * blocks, blocks, 0)
        return code.astype(F32).reshape(blocks, per, kv) * scale[:, None, None]

    old = lax.dynamic_slice_in_dim(weight, x * piece, piece, 0).astype(F32)
    state = jnp.stack(
        [
            decoded(moment_codes, moment_scale),
            decoded(second_codes, second_scale),
            old.reshape(blocks, per, kv),
        ]
    )
    state = jnp.where(c == zh, state, lax.ppermute(state, ("zl", "c", "zh"), CROSS))

    got = a2a(pack(tokens, cotangent), "x").reshape(X * tok, chip + kv)
    got, state, old_half = lax.optimization_barrier((got, state, old_half))
    old_half = lax.all_gather(old_half, "y", axis=0, tiled=True)
    cot = got[:, chip:]
    mine = lax.dynamic_slice_in_dim(got, c * half, half, 1)
    other = lax.dynamic_slice_in_dim(got, (1 - c) * half, half, 1)
    contract = (((0,), (0,)), ((), ()))
    away = lax.dot_general(other, cot, contract, preferred_element_type=F32).astype(BF16)
    away = lax.ppermute(away, "c", SWAP)
    grad = lax.dot_general(mine, cot, contract, preferred_element_type=F32) + away.astype(F32)
    grad = a2a(grad.astype(BF16).reshape(Y, piece, kv), "y")
    grad = jnp.sum(grad.astype(F32), axis=0).astype(BF16)
    grad = jnp.sum(to_all(grad, ("zl", "zh"), ZL * ZH).astype(F32), axis=0) / DP

    grad = grad.reshape(blocks, per, kv)
    moment, second, old = state[0], state[1], state[2]
    moment_new = beta_one * moment + (1.0 - beta_one) * grad
    second_new = beta_two * second + (1.0 - beta_two) * grad * grad
    new = (old - learn_rate * moment_new / (jnp.sqrt(second_new) + adam_eps)).astype(BF16)
    moment_top = jnp.max(jnp.abs(moment_new), axis=(1, 2), keepdims=True) + scale_eps
    second_top = jnp.max(jnp.abs(second_new), axis=(1, 2), keepdims=True) + scale_eps
    codes = jnp.stack([moment_new / moment_top, second_new / second_top]).astype(BF16)
    codes = codes.reshape(2 * piece, kv)

    new = to_all(new.reshape(piece, kv), "y", Y).reshape(half, kv)
    codes = jnp.where(c == zh, codes, lax.ppermute(codes, "c", SWAP))
    new, codes = lax.optimization_barrier((new, codes))
    new_other = lax.ppermute(new, "c", SWAP)
    part = jnp.dot(mine, new, preferred_element_type=F32)
    part = part + jnp.dot(other, new_other, preferred_element_type=F32)
    part = part.astype(BF16).reshape(X, tok, kv)
    codes = jnp.broadcast_to(codes[None], (X,) + codes.shape)
    part = a2a(jnp.concatenate([part, codes], axis=1), "x")

    old_all = in_order(c, old_half, lax.ppermute(old_half, "c", SWAP), 1)
    input_grad = lax.dot_general(
        cotangent, old_all, (((1,), (1,)), ((), ())), preferred_element_type=F32
    ).astype(BF16)

    part, input_grad = lax.optimization_barrier((part, input_grad))
    values = jnp.sum(part[:, :tok].astype(F32), axis=0).astype(BF16)
    codes = part[:, tok:].reshape(X, 2, piece, kv)
    moment_out = codes[:, 0].reshape(rows, kv)
    second_out = codes[:, 1].reshape(rows, kv)
    return (input_grad, values, moment_out, second_out)


def solution(mesh):
    fine = Mesh(mesh.devices.reshape(X, ZL, C, Y, ZH), AXES)
    tokens, state = P(AXES, None), P(("y", "zh"), None)
    scale = P(("y", "zh"))
    return jax.shard_map(
        local,
        mesh=fine,
        in_specs=(tokens, tokens, state, state, scale, state, scale),
        out_specs=(tokens, tokens, state, state),
        check_vma=False,
    )
```

```python
import jax
import jax.numpy as jnp
from jax import lax
from jax.experimental import pallas as pl
from jax.sharding import Mesh
from jax.sharding import PartitionSpec as P

beta_one = 0.9
beta_two = 0.95
learn_rate = 0.004
adam_eps = 1e-08
scale_eps = 1e-06

X, ZL, C, Y, ZH = 4, 4, 2, 8, 2
XS, YS = ("x1", "x0"), ("y2", "y1", "y0")
AXES = XS + ("zl", "c") + YS + ("zh",)
ALONG_X = ("x0", "x1")
ALONG_Y = ("y1", "y0", "y2")
ALONG_Z = ("zl", "zh")
DP = X * ZL * C
F32, BF16 = jnp.float32, jnp.bfloat16

SWAP = [(0, 1), (1, 0)]
CROSS = [
    ((a * C + h) * ZH + h, ((ZL - 1 - a) * C + h) * ZH + 1 - h) for h in range(ZH) for a in range(ZL)
]


def places(axes):
    bits = [int(name[1]) for name in axes]
    top = len(bits) - 1
    return [
        sum((place >> (top - i) & 1) << bit for i, bit in enumerate(bits))
        for place in range(2 ** len(bits))
    ]


def a2a(a, axes):
    return lax.all_to_all(a, axes, 0, 0, tiled=True)


def to_all(a, axes, n):
    return a2a(jnp.broadcast_to(a[None], (n,) + a.shape), axes)


def in_order(index, mine, other, axis):
    return jnp.where(
        index == 0,
        jnp.concatenate([mine, other], axis=axis),
        jnp.concatenate([other, mine], axis=axis),
    )


def pack_kernel(tok_ref, cot_ref, out_ref):
    shard = tok_ref.shape[1] // (Y * ZH)
    run = shard // X
    ys = places(ALONG_Y)
    for to, x in enumerate(places(ALONG_X)):
        for h in range(ZH):
            for at in range(0, Y, 2):
                both = [
                    tok_ref[:, pl.ds((y * ZH + h) * shard + x * run, run)] for y in ys[at : at + 2]
                ]
                out_ref[to, :, pl.ds((h * Y + at) * run, 2 * run)] = jnp.concatenate(both, axis=1)
        out_ref[to, :, pl.ds(ZH * Y * run, cot_ref.shape[1])] = cot_ref[...]


def pack(tokens, cotangent):
    tok, dw = tokens.shape
    kv = cotangent.shape[1]
    block = tok // 2
    wide = dw // X + kv
    return pl.pallas_call(
        pack_kernel,
        grid=(tok // block,),
        in_specs=[
            pl.BlockSpec((block, dw), lambda i: (i, 0)),
            pl.BlockSpec((block, kv), lambda i: (i, 0)),
        ],
        out_specs=pl.BlockSpec((X, block, wide), lambda i: (0, i, 0)),
        out_shape=jax.ShapeDtypeStruct((X, tok, wide), BF16),
        cost_estimate=pl.CostEstimate(
            flops=0, bytes_accessed=2 * tok * (dw + kv + X * wide), transcendentals=0
        ),
    )(tokens, cotangent)


def local(tokens, cotangent, weight, moment_codes, moment_scale, second_codes, second_scale):
    x, c, zh = (lax.axis_index(name) for name in (XS, "c", "zh"))
    rows, kv = weight.shape
    tok, dw = tokens.shape
    chip = dw // X
    half = chip // C
    piece = half // Y
    per = 2048 // kv
    blocks = piece // per

    old_half = lax.dynamic_slice_in_dim(weight, c * (kv // 2), kv // 2, 1)
    old_half = in_order(zh, old_half, lax.ppermute(old_half, "zh", SWAP), 0)

    def decoded(code, scale):
        code = lax.dynamic_slice_in_dim(code, x * piece, piece, 0)
        scale = lax.dynamic_slice_in_dim(scale, x * blocks, blocks, 0)
        return code.astype(F32).reshape(blocks, per, kv) * scale[:, None, None]

    old = lax.dynamic_slice_in_dim(weight, x * piece, piece, 0).astype(F32)
    state = jnp.stack(
        [
            decoded(moment_codes, moment_scale),
            decoded(second_codes, second_scale),
            old.reshape(blocks, per, kv),
        ]
    )
    state = jnp.where(c == zh, state, lax.ppermute(state, ("zl", "c", "zh"), CROSS))

    got = a2a(pack(tokens, cotangent), ALONG_X).reshape(X * tok, chip + kv)
    got, state, old_half = lax.optimization_barrier((got, state, old_half))
    old_half = lax.all_gather(old_half, YS, axis=0, tiled=True)
    cot = got[:, chip:]
    mine = lax.dynamic_slice_in_dim(got, c * half, half, 1)
    other = lax.dynamic_slice_in_dim(got, (1 - c) * half, half, 1)
    contract = (((0,), (0,)), ((), ()))
    away = lax.dot_general(other, cot, contract, preferred_element_type=F32).astype(BF16)
    away = lax.ppermute(away, "c", SWAP)
    grad = lax.dot_general(mine, cot, contract, preferred_element_type=F32) + away.astype(F32)
    grad = a2a(grad.astype(BF16).reshape(Y, piece, kv), ALONG_Y)
    grad = jnp.sum(grad.astype(F32), axis=0).astype(BF16)
    grad = jnp.sum(to_all(grad, ALONG_Z, ZL * ZH).astype(F32), axis=0) / DP

    grad = grad.reshape(blocks, per, kv)
    moment, second, old = state[0], state[1], state[2]
    moment_new = beta_one * moment + (1.0 - beta_one) * grad
    second_new = beta_two * second + (1.0 - beta_two) * grad * grad
    new = (old - learn_rate * moment_new / (jnp.sqrt(second_new) + adam_eps)).astype(BF16)
    moment_top = jnp.max(jnp.abs(moment_new), axis=(1, 2), keepdims=True) + scale_eps
    second_top = jnp.max(jnp.abs(second_new), axis=(1, 2), keepdims=True) + scale_eps
    codes = jnp.stack([moment_new / moment_top, second_new / second_top]).astype(BF16)
    codes = codes.reshape(2 * piece, kv)

    new = to_all(new.reshape(piece, kv), ALONG_Y, Y).reshape(half, kv)
    codes = jnp.where(c == zh, codes, lax.ppermute(codes, "c", SWAP))
    new, codes = lax.optimization_barrier((new, codes))
    new_other = lax.ppermute(new, "c", SWAP)
    part = jnp.dot(mine, new, preferred_element_type=F32)
    part = part + jnp.dot(other, new_other, preferred_element_type=F32)
    part = part.astype(BF16).reshape(X, tok, kv)
    codes = jnp.broadcast_to(codes[None], (X,) + codes.shape)
    part = a2a(jnp.concatenate([part, codes], axis=1), ALONG_X)

    old_all = in_order(c, old_half, lax.ppermute(old_half, "c", SWAP), 1)
    input_grad = lax.dot_general(
        cotangent, old_all, (((1,), (1,)), ((), ())), preferred_element_type=F32
    ).astype(BF16)

    part, input_grad = lax.optimization_barrier((part, input_grad))
    values = jnp.sum(part[:, :tok].astype(F32), axis=0).astype(BF16)
    codes = part[:, tok:].reshape(X, 2, piece, kv)
    xs = places(ALONG_X)
    codes = jnp.concatenate([codes[xs.index(i)] for i in range(X)], axis=1)
    moment_out, second_out = codes[0], codes[1]
    return (input_grad, values, moment_out, second_out)


def solution(mesh):
    fine = Mesh(mesh.devices.reshape(2, 2, ZL, C, 2, 2, 2, ZH), AXES)
    tokens, state = P(AXES, None), P(YS + ("zh",), None)
    scale = P(YS + ("zh",))
    return jax.shard_map(
        local,
        mesh=fine,
        in_specs=(tokens, tokens, state, state, scale, state, scale),
        out_specs=(tokens, tokens, state, state),
        check_vma=False,
    )
```

```python
import jax
import jax.numpy as jnp
from jax import lax
from jax.experimental import pallas as pl
from jax.sharding import Mesh
from jax.sharding import PartitionSpec as P

beta_one = 0.9
beta_two = 0.95
learn_rate = 0.004
adam_eps = 1e-08
scale_eps = 1e-06

X, ZL, C, Y, ZH = 4, 4, 2, 8, 2
XS, YS = ("x1", "x0"), ("y2", "y1", "y0")
AXES = XS + ("zl", "c") + YS + ("zh",)
ALONG_X = ("x0", "x1")
ALONG_Y = ("y1", "y0", "y2")
ALONG_Z = ("zl", "zh")
DP = X * ZL * C
F32, BF16 = jnp.float32, jnp.bfloat16

SWAP = [(0, 1), (1, 0)]
CROSS = [
    ((a * C + h) * ZH + h, ((ZL - 1 - a) * C + h) * ZH + 1 - h) for h in range(ZH) for a in range(ZL)
]


def places(axes):
    bits = [int(name[1]) for name in axes]
    top = len(bits) - 1
    return [
        sum((place >> (top - i) & 1) << bit for i, bit in enumerate(bits))
        for place in range(2 ** len(bits))
    ]


def a2a(a, axes):
    return lax.all_to_all(a, axes, 0, 0, tiled=True)


def to_all(a, axes, n):
    return a2a(jnp.broadcast_to(a[None], (n,) + a.shape), axes)


def in_order(index, mine, other, axis):
    return jnp.where(
        index == 0,
        jnp.concatenate([mine, other], axis=axis),
        jnp.concatenate([other, mine], axis=axis),
    )


def pack_kernel(tok_ref, cot_ref, out_ref):
    shard = tok_ref.shape[1] // (Y * ZH)
    run = shard // X
    ys = places(ALONG_Y)
    for to, x in enumerate(places(ALONG_X)):
        for h in range(ZH):
            for at in range(0, Y, 2):
                both = [
                    tok_ref[:, pl.ds((y * ZH + h) * shard + x * run, run)] for y in ys[at : at + 2]
                ]
                out_ref[to, :, pl.ds((h * Y + at) * run, 2 * run)] = jnp.concatenate(both, axis=1)
        out_ref[to, :, pl.ds(ZH * Y * run, cot_ref.shape[1])] = cot_ref[...]


def pack(tokens, cotangent):
    tok, dw = tokens.shape
    kv = cotangent.shape[1]
    block = tok // 2
    wide = dw // X + kv
    return pl.pallas_call(
        pack_kernel,
        grid=(tok // block,),
        in_specs=[
            pl.BlockSpec((block, dw), lambda i: (i, 0)),
            pl.BlockSpec((block, kv), lambda i: (i, 0)),
        ],
        out_specs=pl.BlockSpec((X, block, wide), lambda i: (0, i, 0)),
        out_shape=jax.ShapeDtypeStruct((X, tok, wide), BF16),
        cost_estimate=pl.CostEstimate(
            flops=0, bytes_accessed=2 * tok * (dw + kv + X * wide), transcendentals=0
        ),
    )(tokens, cotangent)


def local(tokens, cotangent, weight, moment_codes, moment_scale, second_codes, second_scale):
    x, c, zh = (lax.axis_index(name) for name in (XS, "c", "zh"))
    rows, kv = weight.shape
    tok, dw = tokens.shape
    chip = dw // X
    half = chip // C
    piece = half // Y
    per = 2048 // kv
    blocks = piece // per

    old_half = lax.dynamic_slice_in_dim(weight, c * (kv // 2), kv // 2, 1)
    old_half = in_order(zh, old_half, lax.ppermute(old_half, "zh", SWAP), 0)

    def decoded(code, scale):
        code = lax.dynamic_slice_in_dim(code, x * piece, piece, 0)
        scale = lax.dynamic_slice_in_dim(scale, x * blocks, blocks, 0)
        return code.astype(F32).reshape(blocks, per, kv) * scale[:, None, None]

    old = lax.dynamic_slice_in_dim(weight, x * piece, piece, 0).astype(F32)
    state = jnp.stack(
        [
            decoded(moment_codes, moment_scale),
            decoded(second_codes, second_scale),
            old.reshape(blocks, per, kv),
        ]
    )
    state = jnp.where(c == zh, state, lax.ppermute(state, ("zl", "c", "zh"), CROSS))

    got = a2a(pack(tokens, cotangent), ALONG_X).reshape(X * tok, chip + kv)
    got, state, old_half = lax.optimization_barrier((got, state, old_half))
    old_half = lax.all_gather(old_half, YS, axis=0, tiled=True)
    cot = got[:, chip:]
    mine = lax.dynamic_slice_in_dim(got, c * half, half, 1)
    other = lax.dynamic_slice_in_dim(got, (1 - c) * half, half, 1)
    contract = (((0,), (0,)), ((), ()))
    away = lax.dot_general(other, cot, contract, preferred_element_type=F32).astype(BF16)
    away = lax.ppermute(away, "c", SWAP)
    kept = lax.dot_general(mine, cot, contract, preferred_element_type=F32)
    kept, away = lax.optimization_barrier((kept, away))
    grad = kept + away.astype(F32)
    grad = a2a(grad.astype(BF16).reshape(Y, piece, kv), ALONG_Y)
    grad = jnp.sum(grad.astype(F32), axis=0).astype(BF16)
    grad = jnp.sum(to_all(grad, ALONG_Z, ZL * ZH).astype(F32), axis=0) / DP

    grad = grad.reshape(blocks, per, kv)
    moment, second, old = state[0], state[1], state[2]
    moment_new = beta_one * moment + (1.0 - beta_one) * grad
    second_new = beta_two * second + (1.0 - beta_two) * grad * grad
    new = (old - learn_rate * moment_new / (jnp.sqrt(second_new) + adam_eps)).astype(BF16)
    moment_top = jnp.max(jnp.abs(moment_new), axis=(1, 2), keepdims=True) + scale_eps
    second_top = jnp.max(jnp.abs(second_new), axis=(1, 2), keepdims=True) + scale_eps
    codes = jnp.stack([moment_new / moment_top, second_new / second_top]).astype(BF16)
    codes = codes.reshape(2 * piece, kv)

    new = to_all(new.reshape(piece, kv), ALONG_Y, Y).reshape(half, kv)
    codes = jnp.where(c == zh, codes, lax.ppermute(codes, "c", SWAP))
    new, codes = lax.optimization_barrier((new, codes))
    new_other = lax.ppermute(new, "c", SWAP)
    part = jnp.dot(mine, new, preferred_element_type=F32)
    part = part + jnp.dot(other, new_other, preferred_element_type=F32)
    part = part.astype(BF16).reshape(X, tok, kv)
    codes = jnp.broadcast_to(codes[None], (X,) + codes.shape)
    part = a2a(jnp.concatenate([part, codes], axis=1), ALONG_X)

    old_all = in_order(c, old_half, lax.ppermute(old_half, "c", SWAP), 1)
    input_grad = lax.dot_general(
        cotangent, old_all, (((1,), (1,)), ((), ())), preferred_element_type=F32
    ).astype(BF16)

    part, input_grad = lax.optimization_barrier((part, input_grad))
    values = jnp.sum(part[:, :tok].astype(F32), axis=0).astype(BF16)
    codes = part[:, tok:].reshape(X, 2, piece, kv)
    xs = places(ALONG_X)
    codes = jnp.concatenate([codes[xs.index(i)] for i in range(X)], axis=1)
    moment_out, second_out = codes[0], codes[1]
    return (input_grad, values, moment_out, second_out)


def solution(mesh):
    fine = Mesh(mesh.devices.reshape(2, 2, ZL, C, 2, 2, 2, ZH), AXES)
    tokens, state = P(AXES, None), P(YS + ("zh",), None)
    scale = P(YS + ("zh",))
    return jax.shard_map(
        local,
        mesh=fine,
        in_specs=(tokens, tokens, state, state, scale, state, scale),
        out_specs=(tokens, tokens, state, state),
        check_vma=False,
    )
```
